256 devices in a mesh: dp: 32 (over y, z), mp: 8 (over x, core).
Axes of the slice: x: 4, y: 4, z: 8, core: 2. Of those that a mesh axis runs over, the one named last changes fastest.
Arguments:
- grads: bfloat16 [512, 512, 512], P('dp', 'mp'), may hold values from -0.25 to 0.25
- old_stat: float32 [512, 512, 512], P('dp', 'mp'), as said below
- counts: int32 [32], replicated, may hold values from 1 to 16, 256 in all
Outputs:
- new_stat: float32 [512, 512, 512], P('dp', 'mp')
- roots: bfloat16 [512, 512, 512], P('dp', 'mp')
The draws below stay inside these ranges and needn't reach their ends.
Inputs may be any that keep to these rules, and one draw needn't show every extreme that they name: The counts sum to 256, and the largest is exactly 16. `old_stat`: every block is symmetric and positive definite.
All inputs are finite; a program needn't handle non-finite values.
Results may differ from the reference program's by a relative error of at most 0.005.
Values may be sent and summed in bfloat16 or wider, within the bound.
A program may use at most 128 MiB of HBM per device.

```python
import math
import jax
import jax.numpy as jnp
import numpy as np
from jax import lax

BLOCK_ORDER = 512
ITERS = 5
GRADIENT_ROWS = 512
OWN = 16
SLOT_COUNT = 512
TOTAL = 256
N_DP = 32


def draw_old_stat(key, part):
    key = jax.random.fold_in(key, 7)
    key_diagonal, key_perturbation, key_vector, key_strength = jax.random.split(key, 4)
    log_upper_bound = math.log(8.0)
    diagonal_values = jnp.exp(jax.random.uniform(key_diagonal, (SLOT_COUNT, BLOCK_ORDER), jnp.float32, 0.0, log_upper_bound))
    perturbation = jax.random.uniform(key_perturbation, (SLOT_COUNT, BLOCK_ORDER, BLOCK_ORDER), jnp.float32, -1.0, 1.0)
    symmetric = 0.5 * (perturbation + jnp.swapaxes(perturbation, 1, 2))
    root_diag = jnp.sqrt(diagonal_values)
    off_part = 0.9 / BLOCK_ORDER * root_diag[:, :, None] * root_diag[:, None, :] * symmetric
    identity = jnp.eye(BLOCK_ORDER, dtype=jnp.float32)
    base = off_part * (1.0 - identity) + diagonal_values[:, :, None] * identity
    direction = jax.random.uniform(key_vector, (SLOT_COUNT, BLOCK_ORDER), jnp.float32, -1.0, 1.0) * math.sqrt(3.0 / BLOCK_ORDER)
    strength = math.sqrt(BLOCK_ORDER) * jnp.exp(jax.random.uniform(key_strength, (SLOT_COUNT,), jnp.float32, 0.0, math.log(40.0)))
    dominant = strength[:, None, None] * direction[:, :, None] * direction[:, None, :]
    return base + dominant


def level_of(own_key, shape, shards, smallest, largest):
    factor_of, own = 1.0, jax.random.fold_in(own_key, 6)
    for position, shards_of in shards:
        steps = jnp.exp(jax.random.uniform(jax.random.fold_in(own, position), (shards_of,), jnp.float32, smallest / len(shards), largest / len(shards)))
        factor_of = factor_of * jnp.repeat(steps, shape[position] // shards_of).reshape([-1 if axis == position else 1 for axis in range(len(shape))])
    return factor_of


def profile(count, total, limit, slope):
    weights = [(1 << 20) // math.isqrt(rank ** slope) + 1 for rank in range(2, count + 1)]
    rest, given = total - limit - (count - 1), [1] * (count - 1)
    while rest > 0:
        candidates = [i for i in range(count - 1) if given[i] < limit]
        mass, left = sum([weights[i] for i in candidates]), rest
        for i in candidates:
            more = min(limit - given[i], max(1, left * weights[i] // mass), rest)
            given[i] = given[i] + more
            rest = rest - more
    return np.array([limit] + given)


def ragged(own_key, amount, total, limit, slope):
    if amount == 2:
        one = jax.random.randint(own_key, (), max(1, total - limit), min(limit, total - 1) + 1)
        return jnp.stack([one, total - one])
    tallies = jnp.asarray(profile(amount, total, limit, slope), jnp.int32)
    couples = (amount - 1) // 2
    source_of, sink = tallies[1:1 + 2 * couples:2], tallies[2:2 + 2 * couples:2]
    room = jnp.minimum(source_of - 1, limit - sink)
    moved = jax.random.randint(jax.random.fold_in(own_key, 1), (couples,), 0, 1 << 20) % (room + 1)
    tallies = tallies.at[1:1 + 2 * couples:2].set(source_of - moved).at[2:2 + 2 * couples:2].set(sink + moved)
    return tallies[jax.random.permutation(jax.random.fold_in(own_key, 2), amount)]


def noise(key, shape, width, bound, cuts=(), held_as=jnp.bfloat16):
    entries = jax.random.normal(key, shape, jnp.float32) * width
    if len(cuts) > 0:
        entries = level_of(key, shape, cuts, -0.22, 0.18) * entries
    return jnp.clip(entries, min=-bound, max=bound).astype(held_as)


def setup_inputs(seed: int = 0) -> dict:
    arg_keys = jax.random.split(jax.random.key(seed), 4)
    return {
        "grads": noise(arg_keys[0], (SLOT_COUNT, GRADIENT_ROWS, BLOCK_ORDER), GRADIENT_ROWS ** -0.5, 0.25, ((0, 32), (1, 8))),
        "old_stat": draw_old_stat(jax.random.fold_in(arg_keys[3], 71), 0),
        "counts": ragged(arg_keys[2], N_DP, TOTAL, OWN, 2).astype(jnp.int32),
    }


decay_rate = 0.5

def newton_roots(blocks):
    order_size = blocks.shape[-1]
    identity = jnp.eye(order_size, dtype=jnp.float32)
    frob_norm = jnp.sqrt(lax.optimization_barrier(jnp.sum(blocks * blocks, axis=(1, 2))) + 1e-06)
    scaling = (2.5 / frob_norm)[:, None, None]
    matrix = scaling * blocks
    approx = scaling ** 0.25 * identity
    for iteration in range(ITERS):
        factor = (5.0 * identity - matrix) * 0.25
        approx = jnp.einsum('nij,njk->nik', approx, factor, precision=lax.Precision.HIGHEST)
        square = jnp.einsum('nij,njk->nik', factor, factor, precision=lax.Precision.HIGHEST)
        fourth = jnp.einsum('nij,njk->nik', square, square, precision=lax.Precision.HIGHEST)
        matrix = jnp.einsum('nij,njk->nik', fourth, matrix, precision=lax.Precision.HIGHEST)
    return approx.astype(jnp.bfloat16)

def reference(grads, old_stat, counts):
    ends = jnp.cumsum(counts).astype(jnp.int32)
    starts = (ends - counts).astype(jnp.int32)
    ranks = jnp.arange(TOTAL, dtype=jnp.int32)
    owner = lax.optimization_barrier(jnp.sum((ends[None, :] <= ranks[:, None]).astype(jnp.int32), axis=1)).astype(jnp.int32)
    slot_ids = (owner * OWN + ranks - starts[owner]).astype(jnp.int32)
    chosen = grads[slot_ids].astype(jnp.float32)
    gram = jnp.einsum('krb,krc->kbc', chosen, chosen, precision=lax.Precision.HIGHEST)
    stats = decay_rate * old_stat[slot_ids] + gram
    new_stat = jnp.zeros(old_stat.shape, jnp.float32).at[slot_ids].set(stats)
    root_blocks = newton_roots(stats)
    roots = jnp.zeros(old_stat.shape, jnp.bfloat16).at[slot_ids].set(root_blocks)
    return (new_stat, roots)
```

```python
import jax
import jax.numpy as jnp
from jax import lax
from jax.experimental import pallas as pl
from jax.experimental.pallas import tpu as pltpu
from jax.sharding import PartitionSpec as P

F32 = jnp.float32
BF16 = jnp.bfloat16
MESH = pl.DeviceIdType.MESH

ITERS = 5
DECAY = 0.5
ORDER = 512
ROWS = 64
OWN = 16
PEERS = 8
PHASES = OWN // PEERS
CHIPS = 4
LANE = 128
PIECES = CHIPS + 1
GRADS, OLD, GRAM, ROOT = range(4)

TAKES = (
    ((0, 4), (2, 5), (2, 3), (1, 3)),
    ((0, 4), (2, 4), (2, 3), (0, 3)),
)
BLOCKS = (
    tuple((0, (q + 2) % 4, q) for q in range(4)) + ((1, 1, 2), (1, 2, 3), (1, 3, 4), (2, 2, 2), (3, 2, 1), (3, 3, 2)),
    tuple((0, (q + 2) % 4, q) for q in range(4)) + ((1, 1, 2), (1, 2, 3), (2, 2, 2), (3, 1, 0), (3, 2, 1), (3, 3, 2)),
)


def dot(a, b):
    return lax.dot_general(a, b, (((1,), (0,)), ((), ())), preferred_element_type=F32)


def dot_rows(a, b):
    return lax.dot_general(a, b, (((0,), (0,)), ((), ())), preferred_element_type=F32)


def tiles(height, width):
    for j in range(ORDER // width):
        for i in range(ORDER // height):
            yield slice(i * height, (i + 1) * height), slice(j * width, (j + 1) * width)


def newton_root(stat, mat, mat16, low, low16, up16, root, root16, out):
    total = jnp.zeros((1, 1), F32)
    for r, c in tiles(256, 512):
        a = stat[r, c]
        total = total + jnp.sum(a * a, keepdims=True)
    scaling = 2.5 / jnp.sqrt(total + 1e-6)
    for r, c in tiles(128, 512):
        m = stat[r, c] * scaling
        mat[r, c] = m
        mat16[r, c] = m.astype(BF16)
        row = lax.broadcasted_iota(jnp.int32, m.shape, 0) + r.start
        column = lax.broadcasted_iota(jnp.int32, m.shape, 1) + c.start
        x = jnp.where(row == column, 1.25, 0.0) - 0.25 * m
        root[r, c] = x
        root16[r, c] = x.astype(BF16)

    def step(_, carry):
        for r, c in tiles(256, 256):
            t = dot(mat16[r, :], mat16[:, c]) * 0.0625 - 0.625 * mat[r, c]
            low[r, c] = t
            low16[r, c] = t.astype(BF16)
        for r, c in tiles(256, 256):
            up16[r, c] = (dot(low16[r, :], low16[:, c]) + 3.125 * low[r, c]).astype(BF16)
        for r, c in tiles(256, 256):
            mat[r, c] = (625.0 / 256.0) * mat[r, c] + dot(up16[r, :], mat16[:, c])
        mat16[...] = mat[...].astype(BF16)
        for r, c in tiles(256, 256):
            root[r, c] = 1.25 * root[r, c] - 0.25 * dot(root16[r, :], mat16[:, c])
        root16[...] = root[...].astype(BF16)
        return carry

    lax.fori_loop(0, ITERS - 1, step, 0)
    quarter = jnp.sqrt(jnp.sqrt(scaling))
    for r, c in tiles(128, 512):
        out[r, c] = (root[r, c] * quarter).astype(BF16)


def kernel(
    grads, old, gram_out, root_out,
    g_in, o_all, o_send, o_in, gram_send, root_send,
    stat, mat, mat16, low, low16, up16, root, root16,
    load_sem, send_sem, recv_sem,
):
    dp = lax.axis_index("dp")
    me = lax.axis_index("mp")
    x, core = me // 2, lax.rem(me, 2)

    loads = [
        pltpu.make_async_copy(old.at[pl.ds(p * PEERS, PEERS)], o_all.at[pl.ds(p * PEERS, PEERS)], load_sem.at[p])
        for p in range(PHASES)
    ]
    for load in loads:
        load.start()

    peers = []
    for dr in range(CHIPS):
        for dc in range(2):
            peers.append((dr, dc, lax.rem(x + CHIPS - dr, CHIPS) * 2 + lax.rem(core + dc, 2)))

    barrier = pltpu.get_barrier_semaphore()
    for _, _, to in peers[1:]:
        pl.semaphore_signal(barrier, inc=1, device_id=(dp, to), device_id_type=MESH)
    pl.semaphore_wait(barrier, PEERS - 1)

    def transfers(kind, p):
        out = []
        for d, (dr, dc, to) in enumerate(peers):
            if kind == GRADS:
                src = grads.at[p * PEERS + to]
                dst = g_in.at[p, pl.ds(pl.multiple_of(me * ROWS, ROWS), ROWS)]
            elif kind == OLD:
                a, b = TAKES[p][dr]
                src = o_send.at[p * PEERS + to, pl.ds(a, b - a)]
                dst = o_in.at[p, dr * 2 + core, pl.ds(a, b - a)]
            elif kind == GRAM:
                src = gram_send.at[p, pl.ds(pl.multiple_of(to * ROWS, ROWS), ROWS)]
                dst = gram_out.at[p * PEERS + me]
            else:
                src = root_send.at[p, pl.ds(pl.multiple_of(to * ROWS, ROWS), ROWS)]
                dst = root_out.at[p * PEERS + me]
            if d == 0:
                out.append(pltpu.make_async_copy(src, dst, recv_sem.at[kind, p, d]))
            else:
                out.append(
                    pltpu.make_async_remote_copy(
                        src_ref=src,
                        dst_ref=dst,
                        send_sem=send_sem.at[kind, p, d],
                        recv_sem=recv_sem.at[kind, p, d],
                        device_id=(dp, to),
                        device_id_type=MESH,
                    )
                )
        return out

    moves = {(kind, p): transfers(kind, p) for kind in range(4) for p in range(PHASES)}

    def start(kind, p):
        for copy in moves[kind, p]:
            copy.start()

    def arrive(kind, p):
        own, *rest = moves[kind, p]
        own.wait()
        for copy in rest:
            copy.wait_recv()

    def stage_old(p):
        loads[p].wait()
        k = slice(p * PEERS, (p + 1) * PEERS)
        for q in range(PIECES):
            columns = pl.ds(pl.multiple_of(lax.rem(x + q + 2, CHIPS) * LANE, LANE), LANE)
            o_send[k, q] = (DECAY * o_all[k, :, columns]).astype(BF16)

    def gram_of(p):
        for r, c in tiles(256, 256):
            part = dot_rows(g_in[p, :, r], g_in[p, :, c])
            stat[r, c] = part
            gram_send[p, r, c] = part.astype(BF16)

    def add_old(p):
        there = [pl.ds(pl.multiple_of(lax.rem(x + r, CHIPS) * LANE, LANE), LANE) for r in range(CHIPS)]
        for r, c, q in BLOCKS[p]:
            block = jnp.concatenate([o_in[p, 2 * r, q], o_in[p, 2 * r + 1, q]], axis=0).astype(F32)
            stat[there[r], there[c]] += block
            if r != c:
                stat[there[c], there[r]] += block.T

    start(GRADS, 0)
    stage_old(0)
    start(OLD, 0)
    stage_old(1)
    arrive(GRADS, 0)
    start(GRADS, 1)
    start(OLD, 1)
    for p in range(PHASES):
        if p:
            arrive(GRADS, p)
        gram_of(p)
        start(GRAM, p)
        arrive(OLD, p)
        add_old(p)
        newton_root(stat, mat, mat16, low, low16, up16, root, root16, root_send.at[p])
        start(ROOT, p)
    for kind in (GRAM, ROOT):
        for p in range(PHASES):
            arrive(kind, p)
    for copies in moves.values():
        for copy in copies[1:]:
            copy.wait_send()


def exchange(grads, old_stat):
    square = (ORDER, ORDER)
    return pl.pallas_call(
        kernel,
        out_shape=[jax.ShapeDtypeStruct((OWN, ROWS, ORDER), BF16)] * 2,
        in_specs=[pl.BlockSpec(memory_space=pl.ANY)] * 2,
        out_specs=[pl.BlockSpec(memory_space=pl.ANY)] * 2,
        scratch_shapes=[
            pltpu.VMEM((PHASES,) + square, BF16),
            pltpu.VMEM((OWN, ROWS, ORDER), F32),
            pltpu.VMEM((OWN, PIECES, ROWS, LANE), BF16),
            pltpu.VMEM((PHASES, PEERS, PIECES, ROWS, LANE), BF16),
            pltpu.VMEM((PHASES,) + square, BF16),
            pltpu.VMEM((PHASES,) + square, BF16),
        ]
        + [pltpu.VMEM(square, d) for d in (F32, F32, BF16, F32, BF16, BF16, F32, BF16)]
        + [
            pltpu.SemaphoreType.DMA((PHASES,)),
            pltpu.SemaphoreType.DMA((4, PHASES, PEERS)),
            pltpu.SemaphoreType.DMA((4, PHASES, PEERS)),
        ],
        compiler_params=pltpu.CompilerParams(
            collective_id=0, has_side_effects=True, vmem_limit_bytes=40 << 20
        ),
        cost_estimate=pl.CostEstimate(flops=36 * 2 * ORDER**3, bytes_accessed=6 << 20, transcendentals=0),
        name="refresh",
    )(grads, old_stat)


def on_device(grads, old_stat, counts):
    gram_rows, root_rows = exchange(grads, old_stat)
    filled = (jnp.arange(OWN, dtype=jnp.int32) < counts[lax.axis_index("dp")])[:, None, None]
    new_rows = jnp.where(filled, DECAY * old_stat + gram_rows.astype(F32), 0.0)
    return new_rows, jnp.where(filled, root_rows, jnp.zeros((), BF16))


def solution(mesh):
    placed = P("dp", "mp", None)
    return jax.shard_map(
        on_device,
        mesh=mesh,
        in_specs=(placed, placed, P()),
        out_specs=(placed, placed),
        check_vma=False,
    )
```

```python
import jax
import jax.numpy as jnp
from jax import lax
from jax.experimental import pallas as pl
from jax.experimental.pallas import tpu as pltpu
from jax.sharding import PartitionSpec as P

F32 = jnp.float32
BF16 = jnp.bfloat16
MESH = pl.DeviceIdType.MESH

ITERS = 5
DECAY = 0.5
ORDER = 512
ROWS = 64
OWN = 16
PEERS = 8
PHASES = OWN // PEERS
CHIPS = 4
LANE = 128
PIECES = CHIPS + 1
HALF = ORDER // 2
KINDS = 7
GRADS, OLD, UPPER, ROWS_NEAR, ROWS_FAR, ROOT_NEAR, ROOT_FAR = range(KINDS)

TAKES = (
    ((0, 4), (2, 5), (2, 3), (1, 3)),
    ((0, 4), (2, 4), (2, 3), (0, 3)),
)
BLOCKS = (
    tuple((0, (q + 2) % 4, q) for q in range(4)) + ((1, 1, 2), (1, 2, 3), (1, 3, 4), (2, 2, 2), (3, 2, 1), (3, 3, 2)),
    tuple((0, (q + 2) % 4, q) for q in range(4)) + ((1, 1, 2), (1, 2, 3), (2, 2, 2), (3, 1, 0), (3, 2, 1), (3, 3, 2)),
)


def dot(a, b):
    return lax.dot_general(a, b, (((1,), (0,)), ((), ())), preferred_element_type=F32)


def dot_rows(a, b):
    return lax.dot_general(a, b, (((0,), (0,)), ((), ())), preferred_element_type=F32)


def tiles(height, width):
    for j in range(ORDER // width):
        for i in range(ORDER // height):
            yield slice(i * height, (i + 1) * height), slice(j * width, (j + 1) * width)


def newton_roots(jobs, work):
    jobs = [job + tuple(ref.at[i] for ref in work) for i, job in enumerate(jobs)]
    scalings = []
    for stat, keep, here, there, out, mat, mat16, low, low16, up16, root, root16 in jobs:
        total = jnp.zeros((1, 1), F32)
        for r, c in tiles(256, 512):
            a = stat[r, c].astype(F32)
            total = total + jnp.sum(a * a, keepdims=True)
        scaling = 2.5 / jnp.sqrt(total + 1e-6)
        scalings.append(scaling)
        for r, c in tiles(128, 512):
            m = stat[r, c].astype(F32) * scaling
            mat[r, c] = m
            mat16[r, c] = m.astype(BF16)
        for i, chip in enumerate((here, there)):
            m = mat[pl.ds(pl.multiple_of(chip * LANE, LANE), LANE), :]
            row = lax.broadcasted_iota(jnp.int32, m.shape, 0) + chip * LANE
            column = lax.broadcasted_iota(jnp.int32, m.shape, 1)
            x = jnp.where(row == column, 1.25, 0.0) - 0.25 * m
            root[i * LANE : (i + 1) * LANE, :] = x
            root16[i * LANE : (i + 1) * LANE, :] = x.astype(BF16)

    first, second = slice(0, HALF), slice(HALF, ORDER)
    upper = ((first, first), (first, second), (second, second))

    def put(ref, r, c, value):
        value = value.astype(BF16)
        ref[r, c] = value
        if r != c:
            ref[c, r] = value.T

    def factors():
        for *_, mat, mat16, low, low16, up16, root, root16 in jobs:
            for r, c in upper:
                t = dot(mat16[r, :], mat16[:, c]) * 0.0625 - 0.625 * mat[r, c]
                low[r, c] = t
                put(low16, r, c, t)
        for *_, mat, mat16, low, low16, up16, root, root16 in jobs:
            for r, c in upper:
                put(up16, r, c, dot(low16[r, :], low16[:, c]) + 3.125 * low[r, c])

    def step(_, carry):
        factors()
        for *_, mat, mat16, low, low16, up16, root, root16 in jobs:
            for r, c in upper:
                mat[r, c] = (625.0 / 256.0) * mat[r, c] + dot(up16[r, :], mat16[:, c])
            for r, c in upper:
                put(mat16, r, c, mat[r, c])
        for *_, mat, mat16, low, low16, up16, root, root16 in jobs:
            for c in (first, second):
                root[:, c] = 1.25 * root[:, c] - 0.25 * dot(root16[...], mat16[:, c])
            root16[...] = root[...].astype(BF16)
        return carry

    lax.fori_loop(0, ITERS - 2, step, 0, unroll=True)
    factors()
    for *_, mat, mat16, low, low16, up16, root, root16 in jobs:
        for c in (first, second):
            low16[first, c] = ((625.0 / 256.0) * root[:, c] + dot(root16[...], up16[:, c])).astype(BF16)
    for scaling, (stat, keep, here, there, out, mat, mat16, low, low16, up16, root, root16) in zip(scalings, jobs):
        quarter = jnp.where(keep, jnp.sqrt(jnp.sqrt(scaling)), 0.0)
        for c in (first, second):
            out[:, c] = ((1.25 * root[:, c] - 0.25 * dot(low16[first, :], mat16[:, c])) * quarter).astype(BF16)


def kernel(
    counts, grads, old, new_out, root_out,
    g_in, o_all, o_send, o_in, stat, full, upper_in, rows_in, new, root_send,
    mat, mat16, low, low16, up16, root, root16,
    load_sem, store_sem, send_sem, recv_sem,
):
    dp = lax.axis_index("dp")
    me = lax.axis_index("mp")
    x, core = me // 2, lax.rem(me, 2)
    turn = 1 - 2 * core
    ahead, behind = lax.rem(x + turn + CHIPS, CHIPS), lax.rem(x - turn + CHIPS, CHIPS)
    served = behind * 2 + core

    filled = counts[dp]
    loads = [
        pltpu.make_async_copy(old.at[pl.ds(p * PEERS, PEERS)], o_all.at[pl.ds(p * PEERS, PEERS)], load_sem.at[p])
        for p in range(PHASES)
    ]
    for load in loads:
        load.start()

    peers = []
    for dr in range(CHIPS):
        for dc in range(2):
            peers.append((dr, dc, lax.rem(x + CHIPS - dr, CHIPS) * 2 + lax.rem(core + dc, 2)))

    barrier = pltpu.get_barrier_semaphore()
    for _, _, to in peers[1:]:
        pl.semaphore_signal(barrier, inc=1, device_id=(dp, to), device_id_type=MESH)
    pl.semaphore_wait(barrier, PEERS - 1)

    moves = {}

    def add(kind, p, src, dst, to):
        copies = moves.setdefault((kind, p), [])
        i = len(copies)
        if to is None:
            copies.append((True, pltpu.make_async_copy(src, dst, recv_sem.at[kind, p, i])))
        else:
            copy = pltpu.make_async_remote_copy(
                src_ref=src,
                dst_ref=dst,
                send_sem=send_sem.at[kind, p, i],
                recv_sem=recv_sem.at[kind, p, i],
                device_id=(dp, to),
                device_id_type=MESH,
            )
            copies.append((False, copy))

    def rows(device):
        return pl.ds(pl.multiple_of(device * ROWS, ROWS), ROWS)

    for p in range(PHASES):
        for d, (dr, dc, to) in enumerate(peers):
            target = to if d else None
            a, b = TAKES[p][dr]
            add(GRADS, p, grads.at[p * PEERS + to], g_in.at[p, rows(me)], target)
            add(OLD, p, o_send.at[p * PEERS + to, pl.ds(a, b - a)], o_in.at[p, dr * 2 + core, pl.ds(a, b - a)], target)
        for i in range(CHIPS):
            part = (p, slice(i * LANE, (i + 1) * LANE), slice(i * LANE, ORDER))
            add(UPPER, p, full.at[part], upper_in.at[part], ahead * 2 + core)
        for far, chip, block, k in ((0, behind, full, p * PEERS + me), (1, ahead, upper_in, p * PEERS + served)):
            targets = ((me, None, core), (x * 2 + 1 - core,) * 2 + (1 - core,))
            targets += ((chip * 2 + core,) * 2 + (2 + core,), (chip * 2 + 1 - core,) * 2 + (3 - core,))
            for device, target, piece in targets:
                add(ROWS_NEAR + far, p, block.at[p, rows(device)], rows_in.at[k], target)
                add(ROOT_NEAR + far, p, root_send.at[far, p, rows(piece)], root_out.at[k], target)

    def start(kind, p):
        for _, copy in moves[kind, p]:
            copy.start()

    def arrive(kind, p):
        for local, copy in moves[kind, p]:
            if local:
                copy.wait()
            else:
                copy.wait_recv()

    def stage_old(p):
        loads[p].wait()
        k = slice(p * PEERS, (p + 1) * PEERS)
        for q in range(PIECES):
            columns = pl.ds(pl.multiple_of(lax.rem(x + q + 2, CHIPS) * LANE, LANE), LANE)
            o_send[k, q] = (DECAY * o_all[k, :, columns]).astype(BF16)

    def gram_of(p):
        for r, c in tiles(256, 256):
            stat[p, r, c] = dot_rows(g_in[p, :, r], g_in[p, :, c])

    def add_old(p):
        there = [pl.ds(pl.multiple_of(lax.rem(x + r, CHIPS) * LANE, LANE), LANE) for r in range(CHIPS)]
        for r, c, q in BLOCKS[p]:
            block = jnp.concatenate([o_in[p, 2 * r, q], o_in[p, 2 * r + 1, q]], axis=0).astype(F32)
            stat[p, there[r], there[c]] += block
            if r != c:
                stat[p, there[c], there[r]] += block.T
        full[p] = stat[p].astype(BF16)

    work = (mat, mat16, low, low16, up16, root, root16)

    def near(p):
        return stat.at[p], p * PEERS + me < filled, x, behind, root_send.at[0, p]

    def far(p):
        return upper_in.at[p], p * PEERS + served < filled, x, ahead, root_send.at[1, p]

    def mirror(p):
        arrive(UPPER, p)
        for r in range(CHIPS):
            for c in range(r + 1, CHIPS):
                a, b = slice(r * LANE, (r + 1) * LANE), slice(c * LANE, (c + 1) * LANE)
                upper_in[p, b, a] = upper_in[p, a, b].T
        start(ROWS_FAR, p)

    stores = [
        pltpu.make_async_copy(new.at[pl.ds(p * PEERS, PEERS)], new_out.at[pl.ds(p * PEERS, PEERS)], store_sem.at[p])
        for p in range(PHASES)
    ]

    def refresh_rows(p):
        arrive(ROWS_NEAR, p)
        arrive(ROWS_FAR, p)
        for k in range(p * PEERS, (p + 1) * PEERS):
            decayed = DECAY * o_all[k]
            rest = decayed - decayed.astype(BF16).astype(F32)
            new[k] = jnp.where(k < filled, rows_in[k].astype(F32) + rest, 0.0)
        stores[p].start()

    start(GRADS, 0)
    stage_old(0)
    start(OLD, 0)
    stage_old(1)
    arrive(GRADS, 0)
    start(GRADS, 1)
    gram_of(0)
    arrive(OLD, 0)
    start(OLD, 1)
    add_old(0)
    newton_roots([near(0)], work)
    start(UPPER, 0)
    arrive(GRADS, 1)
    gram_of(1)
    arrive(OLD, 1)
    add_old(1)
    start(UPPER, 1)
    newton_roots([near(1)], work)
    mirror(0)
    start(ROWS_NEAR, 0)
    start(ROOT_NEAR, 0)
    newton_roots([far(0)], work)
    start(ROOT_FAR, 0)
    mirror(1)
    start(ROWS_NEAR, 1)
    start(ROOT_NEAR, 1)
    refresh_rows(0)
    newton_roots([far(1)], work)
    start(ROOT_FAR, 1)
    refresh_rows(1)
    for p in range(PHASES):
        arrive(ROOT_NEAR, p)
        arrive(ROOT_FAR, p)
        stores[p].wait()
    for copies in moves.values():
        for local, copy in copies:
            if not local:
                copy.wait_send()


def exchange(counts, grads, old_stat):
    square = (ORDER, ORDER)
    half = (HALF, ORDER)
    return pl.pallas_call(
        kernel,
        out_shape=[jax.ShapeDtypeStruct((OWN, ROWS, ORDER), d) for d in (F32, BF16)],
        in_specs=[pl.BlockSpec(memory_space=pltpu.SMEM)] + [pl.BlockSpec(memory_space=pltpu.HBM)] * 2,
        out_specs=[pl.BlockSpec(memory_space=pl.ANY)] * 2,
        scratch_shapes=[
            pltpu.VMEM((PHASES,) + square, BF16),
            pltpu.VMEM((OWN, ROWS, ORDER), F32),
            pltpu.VMEM((OWN, PIECES, ROWS, LANE), BF16),
            pltpu.VMEM((PHASES, PEERS, PIECES, ROWS, LANE), BF16),
            pltpu.VMEM((PHASES,) + square, F32),
            pltpu.VMEM((PHASES,) + square, BF16),
            pltpu.VMEM((PHASES,) + square, BF16),
            pltpu.VMEM((OWN, ROWS, ORDER), BF16),
            pltpu.VMEM((OWN, ROWS, ORDER), F32),
            pltpu.VMEM((2, PHASES) + half, BF16),
        ]
        + [pltpu.VMEM((2,) + square, d) for d in (F32, BF16, F32, BF16, BF16)]
        + [pltpu.VMEM((2,) + half, d) for d in (F32, BF16)]
        + [
            pltpu.SemaphoreType.DMA((PHASES,)),
            pltpu.SemaphoreType.DMA((PHASES,)),
            pltpu.SemaphoreType.DMA((KINDS, PHASES, PEERS)),
            pltpu.SemaphoreType.DMA((KINDS, PHASES, PEERS)),
        ],
        compiler_params=pltpu.CompilerParams(
            collective_id=0, has_side_effects=True, vmem_limit_bytes=61 << 20
        ),
        cost_estimate=pl.CostEstimate(flops=60 * 2 * ORDER**3, bytes_accessed=6 << 20, transcendentals=0),
        name="refresh",
    )(counts, grads, old_stat)


def copy_out_kernel(new, root, new_out, root_out, new_held, root_held, load_sem, store_sem):
    loads, stores = [], []
    for i in range(CUTS):
        part = pl.ds(i * (OWN // CUTS), OWN // CUTS)
        for a, (src, held, dst) in enumerate(((new, new_held, new_out), (root, root_held, root_out))):
            loads.append(pltpu.make_async_copy(src.at[part], held.at[part], load_sem.at[a, i]))
            stores.append(pltpu.make_async_copy(held.at[part], dst.at[part], store_sem.at[a, i]))
    for load in loads:
        load.start()
    for load, store in zip(loads, stores):
        load.wait()
        store.start()
    for store in stores:
        store.wait()


CUTS = 4


def copy_out(new, root):
    return pl.pallas_call(
        copy_out_kernel,
        out_shape=[jax.ShapeDtypeStruct(a.shape, a.dtype) for a in (new, root)],
        in_specs=[pl.BlockSpec(memory_space=pl.ANY)] * 2,
        out_specs=[pl.BlockSpec(memory_space=pltpu.HBM)] * 2,
        scratch_shapes=[pltpu.VMEM(a.shape, a.dtype) for a in (new, root)]
        + [pltpu.SemaphoreType.DMA((2, CUTS))] * 2,
        compiler_params=pltpu.CompilerParams(vmem_limit_bytes=61 << 20),
        name="copy_out",
    )(new, root)


def on_device(grads, old_stat, counts):
    return copy_out(*exchange(counts, grads, old_stat))


def solution(mesh):
    placed = P("dp", "mp", None)
    return jax.shard_map(
        on_device,
        mesh=mesh,
        in_specs=(placed, placed, P()),
        out_specs=(placed, placed),
        check_vma=False,
    )
```

```python
import jax
import jax.numpy as jnp
from jax import lax
from jax.experimental import pallas as pl
from jax.experimental.pallas import tpu as pltpu
from jax.sharding import PartitionSpec as P

F32 = jnp.float32
BF16 = jnp.bfloat16
MESH = pl.DeviceIdType.MESH

ITERS = 5
DECAY = 0.5
ORDER = 512
ROWS = 64
OWN = 16
PEERS = 8
PHASES = OWN // PEERS
CHIPS = 4
LANE = 128
PIECES = CHIPS + 1
HALF = ORDER // 2
KINDS = 7
GRADS, OLD, UPPER, ROWS_NEAR, ROWS_FAR, ROOT_NEAR, ROOT_FAR = range(KINDS)

TAKES = (
    ((0, 4), (2, 5), (2, 3), (1, 3)),
    ((0, 4), (2, 4), (2, 3), (0, 3)),
)
BLOCKS = (
    tuple((0, (q + 2) % 4, q) for q in range(4)) + ((1, 1, 2), (1, 2, 3), (1, 3, 4), (2, 2, 2), (3, 2, 1), (3, 3, 2)),
    tuple((0, (q + 2) % 4, q) for q in range(4)) + ((1, 1, 2), (1, 2, 3), (2, 2, 2), (3, 1, 0), (3, 2, 1), (3, 3, 2)),
)


def dot(a, b):
    return lax.dot_general(a, b, (((1,), (0,)), ((), ())), preferred_element_type=F32)


def dot_rows(a, b):
    return lax.dot_general(a, b, (((0,), (0,)), ((), ())), preferred_element_type=F32)


def tiles(height, width):
    for j in range(ORDER // width):
        for i in range(ORDER // height):
            yield slice(i * height, (i + 1) * height), slice(j * width, (j + 1) * width)


def newton_roots(jobs, work):
    jobs = [job + tuple(ref.at[i] for ref in work) for i, job in enumerate(jobs)]
    scalings = []
    for stat, keep, here, there, out, mat, mat16, low, low16, up16, root, root16 in jobs:
        total = jnp.zeros((1, 1), F32)
        for r, c in tiles(256, 512):
            a = stat[r, c].astype(F32)
            total = total + jnp.sum(a * a, keepdims=True)
        scaling = 2.5 / jnp.sqrt(total + 1e-6)
        scalings.append(scaling)
        for r, c in tiles(128, 512):
            m = stat[r, c].astype(F32) * scaling
            mat[r, c] = m
            mat16[r, c] = m.astype(BF16)
        for i, chip in enumerate((here, there)):
            m = mat[pl.ds(pl.multiple_of(chip * LANE, LANE), LANE), :]
            row = lax.broadcasted_iota(jnp.int32, m.shape, 0) + chip * LANE
            column = lax.broadcasted_iota(jnp.int32, m.shape, 1)
            x = jnp.where(row == column, 1.25, 0.0) - 0.25 * m
            root[i * LANE : (i + 1) * LANE, :] = x
            root16[i * LANE : (i + 1) * LANE, :] = x.astype(BF16)

    first, second = slice(0, HALF), slice(HALF, ORDER)
    upper = ((first, first), (first, second), (second, second))

    def put(ref, r, c, value):
        value = value.astype(BF16)
        ref[r, c] = value
        if r != c:
            ref[c, r] = value.T

    def factors():
        for *_, mat, mat16, low, low16, up16, root, root16 in jobs:
            for r, c in upper:
                t = dot(mat16[r, :], mat16[:, c]) * 0.0625 - 0.625 * mat[r, c]
                low[r, c] = t
                put(low16, r, c, t)
        for *_, mat, mat16, low, low16, up16, root, root16 in jobs:
            for r, c in upper:
                put(up16, r, c, dot(low16[r, :], low16[:, c]) + 3.125 * low[r, c])

    def step(_, carry):
        factors()
        for *_, mat, mat16, low, low16, up16, root, root16 in jobs:
            for r, c in upper:
                mat[r, c] = (625.0 / 256.0) * mat[r, c] + dot(up16[r, :], mat16[:, c])
            for r, c in upper:
                put(mat16, r, c, mat[r, c])
        for *_, mat, mat16, low, low16, up16, root, root16 in jobs:
            for c in (first, second):
                root[:, c] = 1.25 * root[:, c] - 0.25 * dot(root16[...], mat16[:, c])
            root16[...] = root[...].astype(BF16)
        return carry

    lax.fori_loop(0, ITERS - 2, step, 0, unroll=True)
    factors()
    for *_, mat, mat16, low, low16, up16, root, root16 in jobs:
        for c in (first, second):
            low16[first, c] = ((625.0 / 256.0) * root[:, c] + dot(root16[...], up16[:, c])).astype(BF16)
    for scaling, (stat, keep, here, there, out, mat, mat16, low, low16, up16, root, root16) in zip(scalings, jobs):
        quarter = jnp.where(keep, jnp.sqrt(jnp.sqrt(scaling)), 0.0)
        for c in (first, second):
            out[:, c] = ((1.25 * root[:, c] - 0.25 * dot(low16[first, :], mat16[:, c])) * quarter).astype(BF16)


def kernel(
    counts, grads, old, new_out, root_out,
    g_in, o_all, o_send, o_in, stat, full, upper_in, rows_in, new, root_send,
    mat, mat16, low, low16, up16, root, root16,
    load_sem, store_sem, send_sem, recv_sem,
):
    dp = lax.axis_index("dp")
    me = lax.axis_index("mp")
    x, core = me // 2, lax.rem(me, 2)
    turn = 1 - 2 * core
    ahead, behind = lax.rem(x + turn + CHIPS, CHIPS), lax.rem(x - turn + CHIPS, CHIPS)
    served = behind * 2 + core

    filled = counts[dp]
    loads = [
        pltpu.make_async_copy(old.at[pl.ds(p * PEERS, PEERS)], o_all.at[pl.ds(p * PEERS, PEERS)], load_sem.at[p])
        for p in range(PHASES)
    ]
    for load in loads:
        load.start()

    peers = []
    for dr in range(CHIPS):
        for dc in range(2):
            peers.append((dr, dc, lax.rem(x + CHIPS - dr, CHIPS) * 2 + lax.rem(core + dc, 2)))

    barrier = pltpu.get_barrier_semaphore()
    for _, _, to in peers[1:]:
        pl.semaphore_signal(barrier, inc=1, device_id=(dp, to), device_id_type=MESH)
    pl.semaphore_wait(barrier, PEERS - 1)

    moves = {}

    def add(kind, p, src, dst, to):
        copies = moves.setdefault((kind, p), [])
        i = len(copies)
        if to is None:
            copies.append((True, pltpu.make_async_copy(src, dst, recv_sem.at[kind, p, i])))
        else:
            copy = pltpu.make_async_remote_copy(
                src_ref=src,
                dst_ref=dst,
                send_sem=send_sem.at[kind, p, i],
                recv_sem=recv_sem.at[kind, p, i],
                device_id=(dp, to),
                device_id_type=MESH,
            )
            copies.append((False, copy))

    def rows(device):
        return pl.ds(pl.multiple_of(device * ROWS, ROWS), ROWS)

    for p in range(PHASES):
        for d, (dr, dc, to) in enumerate(peers):
            target = to if d else None
            a, b = TAKES[p][dr]
            add(GRADS, p, grads.at[p * PEERS + to], g_in.at[p, rows(me)], target)
            add(OLD, p, o_send.at[p * PEERS + to, pl.ds(a, b - a)], o_in.at[p, dr * 2 + core, pl.ds(a, b - a)], target)
        for i in range(CHIPS):
            part = (p, slice(i * LANE, (i + 1) * LANE), slice(i * LANE, ORDER))
            add(UPPER, p, full.at[part], upper_in.at[part], ahead * 2 + core)
        for far, chip, block, k in ((0, behind, full, p * PEERS + me), (1, ahead, upper_in, p * PEERS + served)):
            targets = ((me, None, core), (x * 2 + 1 - core,) * 2 + (1 - core,))
            targets += ((chip * 2 + core,) * 2 + (2 + core,), (chip * 2 + 1 - core,) * 2 + (3 - core,))
            for device, target, piece in targets:
                add(ROWS_NEAR + far, p, block.at[p, rows(device)], rows_in.at[k], target)
                add(ROOT_NEAR + far, p, root_send.at[far, p, rows(piece)], root_out.at[k], target)

    def start(kind, p):
        for _, copy in moves[kind, p]:
            copy.start()

    def arrive(kind, p):
        for local, copy in moves[kind, p]:
            if local:
                copy.wait()
            else:
                copy.wait_recv()

    def stage_old(p):
        loads[p].wait()
        k = slice(p * PEERS, (p + 1) * PEERS)
        for q in range(PIECES):
            columns = pl.ds(pl.multiple_of(lax.rem(x + q + 2, CHIPS) * LANE, LANE), LANE)
            o_send[k, q] = (DECAY * o_all[k, :, columns]).astype(BF16)

    def gram_of(p):
        for r, c in tiles(256, 256):
            stat[p, r, c] = dot_rows(g_in[p, :, r], g_in[p, :, c])

    def add_old(p):
        there = [pl.ds(pl.multiple_of(lax.rem(x + r, CHIPS) * LANE, LANE), LANE) for r in range(CHIPS)]
        for r, c, q in BLOCKS[p]:
            block = jnp.concatenate([o_in[p, 2 * r, q], o_in[p, 2 * r + 1, q]], axis=0).astype(F32)
            stat[p, there[r], there[c]] += block
            if r != c:
                stat[p, there[c], there[r]] += block.T
        full[p] = stat[p].astype(BF16)

    work = (mat, mat16, low, low16, up16, root, root16)

    def near(p):
        return stat.at[p], p * PEERS + me < filled, x, behind, root_send.at[0, p]

    def far(p):
        return upper_in.at[p], p * PEERS + served < filled, x, ahead, root_send.at[1, p]

    def mirror(p):
        arrive(UPPER, p)
        for r in range(CHIPS):
            for c in range(r + 1, CHIPS):
                a, b = slice(r * LANE, (r + 1) * LANE), slice(c * LANE, (c + 1) * LANE)
                upper_in[p, b, a] = upper_in[p, a, b].T
        start(ROWS_FAR, p)

    stores = [
        pltpu.make_async_copy(new.at[pl.ds(p * PEERS, PEERS)], new_out.at[pl.ds(p * PEERS, PEERS)], store_sem.at[p])
        for p in range(PHASES)
    ]

    def refresh_rows(p):
        arrive(ROWS_NEAR, p)
        arrive(ROWS_FAR, p)
        for k in range(p * PEERS, (p + 1) * PEERS):
            decayed = DECAY * o_all[k]
            rest = decayed - decayed.astype(BF16).astype(F32)
            new[k] = jnp.where(k < filled, rows_in[k].astype(F32) + rest, 0.0)
        stores[p].start()

    start(GRADS, 0)
    stage_old(0)
    start(OLD, 0)
    stage_old(1)
    arrive(GRADS, 0)
    start(GRADS, 1)
    gram_of(0)
    arrive(OLD, 0)
    start(OLD, 1)
    add_old(0)
    newton_roots([near(0)], work)
    start(UPPER, 0)
    arrive(GRADS, 1)
    gram_of(1)
    arrive(OLD, 1)
    add_old(1)
    start(UPPER, 1)
    newton_roots([near(1)], work)
    mirror(0)
    start(ROWS_NEAR, 0)
    start(ROOT_NEAR, 0)
    start(ROWS_NEAR, 1)
    start(ROOT_NEAR, 1)
    newton_roots([far(0)], work)
    start(ROOT_FAR, 0)
    mirror(1)
    newton_roots([far(1)], work)
    start(ROOT_FAR, 1)
    refresh_rows(0)
    refresh_rows(1)
    for p in range(PHASES):
        arrive(ROOT_NEAR, p)
        arrive(ROOT_FAR, p)
        stores[p].wait()
    for copies in moves.values():
        for local, copy in copies:
            if not local:
                copy.wait_send()


def exchange(counts, grads, old_stat):
    square = (ORDER, ORDER)
    half = (HALF, ORDER)
    return pl.pallas_call(
        kernel,
        out_shape=[jax.ShapeDtypeStruct((OWN, ROWS, ORDER), d) for d in (F32, BF16)],
        in_specs=[pl.BlockSpec(memory_space=pltpu.SMEM)] + [pl.BlockSpec(memory_space=pltpu.HBM)] * 2,
        out_specs=[pl.BlockSpec(memory_space=pl.ANY)] * 2,
        scratch_shapes=[
            pltpu.VMEM((PHASES,) + square, BF16),
            pltpu.VMEM((OWN, ROWS, ORDER), F32),
            pltpu.VMEM((OWN, PIECES, ROWS, LANE), BF16),
            pltpu.VMEM((PHASES, PEERS, PIECES, ROWS, LANE), BF16),
            pltpu.VMEM((PHASES,) + square, F32),
            pltpu.VMEM((PHASES,) + square, BF16),
            pltpu.VMEM((PHASES,) + square, BF16),
            pltpu.VMEM((OWN, ROWS, ORDER), BF16),
            pltpu.VMEM((OWN, ROWS, ORDER), F32),
            pltpu.VMEM((2, PHASES) + half, BF16),
        ]
        + [pltpu.VMEM((2,) + square, d) for d in (F32, BF16, F32, BF16, BF16)]
        + [pltpu.VMEM((2,) + half, d) for d in (F32, BF16)]
        + [
            pltpu.SemaphoreType.DMA((PHASES,)),
            pltpu.SemaphoreType.DMA((PHASES,)),
            pltpu.SemaphoreType.DMA((KINDS, PHASES, PEERS)),
            pltpu.SemaphoreType.DMA((KINDS, PHASES, PEERS)),
        ],
        compiler_params=pltpu.CompilerParams(
            collective_id=0, has_side_effects=True, vmem_limit_bytes=61 << 20
        ),
        cost_estimate=pl.CostEstimate(flops=60 * 2 * ORDER**3, bytes_accessed=6 << 20, transcendentals=0),
        name="refresh",
    )(counts, grads, old_stat)


def copy_out_kernel(new, root, new_out, root_out, new_held, root_held, load_sem, store_sem):
    loads, stores = [], []
    for i in range(CUTS):
        part = pl.ds(i * (OWN // CUTS), OWN // CUTS)
        for a, (src, held, dst) in enumerate(((new, new_held, new_out), (root, root_held, root_out))):
            loads.append(pltpu.make_async_copy(src.at[part], held.at[part], load_sem.at[a, i]))
            stores.append(pltpu.make_async_copy(held.at[part], dst.at[part], store_sem.at[a, i]))
    for load in loads:
        load.start()
    for load, store in zip(loads, stores):
        load.wait()
        store.start()
    for store in stores:
        store.wait()


CUTS = 4


def copy_out(new, root):
    return pl.pallas_call(
        copy_out_kernel,
        out_shape=[jax.ShapeDtypeStruct(a.shape, a.dtype) for a in (new, root)],
        in_specs=[pl.BlockSpec(memory_space=pl.ANY)] * 2,
        out_specs=[pl.BlockSpec(memory_space=pltpu.HBM)] * 2,
        scratch_shapes=[pltpu.VMEM(a.shape, a.dtype) for a in (new, root)]
        + [pltpu.SemaphoreType.DMA((2, CUTS))] * 2,
        compiler_params=pltpu.CompilerParams(vmem_limit_bytes=61 << 20),
        name="copy_out",
    )(new, root)


def on_device(grads, old_stat, counts):
    return copy_out(*exchange(counts, grads, old_stat))


def solution(mesh):
    placed = P("dp", "mp", None)
    return jax.shard_map(
        on_device,
        mesh=mesh,
        in_specs=(placed, placed, P()),
        out_specs=(placed, placed),
        check_vma=False,
    )
```
